32 devices in a mesh: dp: 1, block: 32 (over z, y, x, core).
Axes of the slice: x: 2, y: 2, z: 4, core: 2. Of those that a mesh axis runs over, the one named last changes fastest.
Arguments:
- tokens: bfloat16 [1024, 8192], P('dp', 'block'), may hold values from -6 to 6
- cotangent: bfloat16 [1024, 8192], P('dp', 'block'), may hold values from -6 to 6
- up_width: bfloat16 [32, 256, 1024], P('block'), may hold values from -0.375 to 0.375
- up_hidden: bfloat16 [256, 128, 128], P('block'), may hold values from -0.5 to 0.5
- down_hidden: bfloat16 [256, 128, 128], P('block'), may hold values from -0.5 to 0.5
- down_width: bfloat16 [32, 1024, 256], P('block'), may hold values from -0.1875 to 0.1875
Outputs:
- layer_out: bfloat16 [1024, 8192], P('dp', 'block')
- tokens_grad: bfloat16 [1024, 8192], P('dp', 'block')
- up_width_grad: float32 [32, 256, 1024], P('block')
- up_hidden_grad: float32 [256, 128, 128], P('block')
- down_hidden_grad: float32 [256, 128, 128], P('block')
- down_width_grad: float32 [32, 1024, 256], P('block')
The draws below stay inside these ranges and needn't reach their ends.
All inputs are finite; a program needn't handle non-finite values.
Results may differ from the reference program's by a relative error of at most 0.014.
Values may be sent and summed in bfloat16 or wider, within the bound.
A program may use at most 64 MiB of HBM per device.

```python
import math
import jax
import jax.numpy as jnp
from jax import lax

BS = 256
Q = 4
TOKENS = 1024
D = 8192
G = 128
N_BLOCK = 32


def level_of(stream_key, extent, cuts, smallest, top_value):
    factor_of, own = 1.0, jax.random.fold_in(stream_key, 6)
    for position, blocks in cuts:
        steps = jnp.exp(jax.random.uniform(jax.random.fold_in(own, position), (blocks,), jnp.float32, smallest / len(cuts), top_value / len(cuts)))
        factor_of = factor_of * jnp.repeat(steps, extent[position] // blocks).reshape([-1 if axis == position else 1 for axis in range(len(extent))])
    return factor_of


def gaussian(key, extent, spread, limit, cuts=(), kind=jnp.bfloat16):
    entries = spread * jax.random.normal(key, extent, jnp.float32)
    if cuts:
        entries = entries * level_of(key, extent, cuts, -0.22, 0.18)
    return jnp.clip(entries, -limit, limit).astype(kind)


def setup_inputs(seed: int = 0) -> dict:
    key_of = jax.random.split(jax.random.key(seed), 7)
    tokens = gaussian(key_of[0], (TOKENS, D), 1.0, 6.0, ((1, 32),))
    cotangent = gaussian(key_of[1], (TOKENS, D), 1.0, 6.0, ((1, 32),))
    up_width = gaussian(key_of[2], (N_BLOCK, BS, Q * BS), BS ** -0.5, 0.375, ((0, 32),))
    up_hidden = gaussian(key_of[3], (BS, G, G), G ** -0.5, 0.5, ((0, 32),))
    down_hidden = gaussian(key_of[4], (BS, G, G), G ** -0.5, 0.5, ((0, 32),))
    down_width = gaussian(key_of[5], (N_BLOCK, Q * BS, BS), (Q * BS) ** -0.5, 0.1875, ((0, 32),))
    return dict(tokens=tokens, cotangent=cotangent, up_width=up_width, up_hidden=up_hidden, down_hidden=down_hidden, down_width=down_width)


def gelu_exact(value):
    return 0.5 * value * (1.0 + jax.scipy.special.erf(value / math.sqrt(2.0)))

def gelu_slope(value):
    return 0.5 * (1.0 + jax.scipy.special.erf(value / math.sqrt(2.0))) + value * jnp.exp(-0.5 * value * value) / math.sqrt(2.0 * math.pi)

def reference(tokens, cotangent, up_width, up_hidden, down_hidden, down_width):
    block_rows = min(512, TOKENS)
    block_count = TOKENS // block_rows
    token_blocks = tokens.reshape(block_count, block_rows, N_BLOCK, BS)
    cot_blocks = cotangent.reshape(block_count, block_rows, N_BLOCK, BS)
    uw32 = up_width.astype(jnp.float32)
    uh32 = up_hidden.astype(jnp.float32)
    dh32 = down_hidden.astype(jnp.float32)
    dw32 = down_width.astype(jnp.float32)

    def one_block(carry, inputs):
        grad_uw, grad_uh, grad_dh, grad_dw = carry
        x_block, c_block = inputs
        x32 = x_block.astype(jnp.float32)
        c32 = c_block.astype(jnp.float32)
        h_full = jnp.einsum('rbi,bic->rbc', x32, uw32).astype(jnp.bfloat16)
        z_full = h_full.reshape(block_rows, N_BLOCK, BS, Q).transpose(0, 2, 1, 3).reshape(block_rows, BS, G)
        pre_act = jnp.einsum('rkg,kgm->rkm', z_full.astype(jnp.float32), uh32)
        active = gelu_exact(pre_act).astype(jnp.bfloat16)
        e_full = jnp.einsum('rkm,kmn->rkn', active.astype(jnp.float32), dh32).astype(jnp.bfloat16)
        f_full = e_full.reshape(block_rows, BS, N_BLOCK, Q).transpose(0, 2, 1, 3).reshape(block_rows, N_BLOCK, BS * Q)
        layer_out = jnp.einsum('rbc,bco->rbo', f_full.astype(jnp.float32), dw32).astype(jnp.bfloat16)
        df_full = jnp.einsum('rbo,bco->rbc', c32, dw32).astype(jnp.bfloat16)
        grad_dw = grad_dw + jnp.einsum('rbc,rbo->bco', f_full.astype(jnp.float32), c32)
        de_full = df_full.reshape(block_rows, N_BLOCK, BS, Q).transpose(0, 2, 1, 3).reshape(block_rows, BS, G)
        de32 = de_full.astype(jnp.float32)
        grad_dh = grad_dh + jnp.einsum('rkm,rkn->kmn', active.astype(jnp.float32), de32)
        act_grad = jnp.einsum('rkn,kmn->rkm', de32, dh32)
        pre_grad = (act_grad * gelu_slope(pre_act)).astype(jnp.bfloat16)
        grad_uh = grad_uh + jnp.einsum('rkg,rkm->kgm', z_full.astype(jnp.float32), pre_grad.astype(jnp.float32))
        dz_full = jnp.einsum('rkm,kgm->rkg', pre_grad.astype(jnp.float32), uh32).astype(jnp.bfloat16)
        dh_full = dz_full.reshape(block_rows, BS, N_BLOCK, Q).transpose(0, 2, 1, 3).reshape(block_rows, N_BLOCK, BS * Q)
        grad_uw = grad_uw + jnp.einsum('rbi,rbc->bic', x32, dh_full.astype(jnp.float32))
        input_grad = jnp.einsum('rbc,bic->rbi', dh_full.astype(jnp.float32), uw32).astype(jnp.bfloat16)
        return ((grad_uw, grad_uh, grad_dh, grad_dw), (layer_out, input_grad))
    start = (jnp.zeros((N_BLOCK, BS, Q * BS), jnp.float32), jnp.zeros((BS, G, G), jnp.float32), jnp.zeros((BS, G, G), jnp.float32), jnp.zeros((N_BLOCK, Q * BS, BS), jnp.float32))
    totals, (outs, grads) = lax.scan(one_block, start, (token_blocks, cot_blocks))
    grad_scale = 1.0 / math.sqrt(TOKENS)
    return (outs.reshape(TOKENS, N_BLOCK * BS), grads.reshape(TOKENS, N_BLOCK * BS), totals[0] * grad_scale, totals[1] * grad_scale, totals[2] * grad_scale, totals[3] * grad_scale)
```

```python
import functools
import math

import jax
import jax.numpy as jnp
from jax import lax
from jax.experimental import pallas as pl
from jax.experimental.pallas import tpu as pltpu
from jax.sharding import PartitionSpec as P


def gelu_exact(value):
    return 0.5 * value * (1.0 + jax.scipy.special.erf(value / math.sqrt(2.0)))


def gelu_slope(value):
    return 0.5 * (1.0 + jax.scipy.special.erf(value / math.sqrt(2.0))) + value * jnp.exp(
        -0.5 * value * value
    ) / math.sqrt(2.0 * math.pi)


def contract_rows(left, right):
    return lax.dot_general(
        left, right, (((0,), (0,)), ((), ())), preferred_element_type=jnp.float32
    )


def contract_cols(left, right):
    return lax.dot_general(
        left, right, (((1,), (1,)), ((), ())), preferred_element_type=jnp.float32
    )


def shards(tokens, cotangent, up_width, up_hidden, down_hidden, down_width):
    row_count = tokens.shape[0]
    block_size = tokens.shape[1]
    expand = up_width.shape[2] // block_size
    grad_scale = 1.0 / math.sqrt(row_count * lax.axis_size("dp"))
    expanded = jnp.dot(tokens, up_width[0], preferred_element_type=jnp.float32).astype(jnp.bfloat16)
    hidden_tiles = lax.all_to_all(
        expanded.reshape(row_count, block_size, expand),
        "block",
        split_axis=1,
        concat_axis=2,
        tiled=True,
    )
    pre_act = jnp.einsum(
        "tkg,kgm->tkm", hidden_tiles, up_hidden, preferred_element_type=jnp.float32
    )
    active = gelu_exact(pre_act).astype(jnp.bfloat16)
    back_rows = jnp.einsum(
        "tkm,kmn->tkn", active, down_hidden, preferred_element_type=jnp.float32
    ).astype(jnp.bfloat16)
    portion = lax.all_to_all(back_rows, "block", split_axis=2, concat_axis=1, tiled=True)
    flattened = portion.reshape(portion.shape[0], block_size * expand)
    gathered_rows = flattened
    layer_out = jnp.dot(flattened, down_width[0], preferred_element_type=jnp.float32).astype(
        jnp.bfloat16
    )
    out_rows_grad = contract_cols(cotangent, down_width[0]).astype(jnp.bfloat16)
    down_width_grad = contract_rows(gathered_rows, cotangent)[None]
    grad_tiles = lax.all_to_all(
        out_rows_grad.reshape(row_count, block_size, expand),
        "block",
        split_axis=1,
        concat_axis=2,
        tiled=True,
    )
    down_hidden_grad = jnp.einsum(
        "tkm,tkn->kmn", active, grad_tiles, preferred_element_type=jnp.float32
    )
    act_grad = jnp.einsum(
        "tkn,kmn->tkm", grad_tiles, down_hidden, preferred_element_type=jnp.float32
    )
    pre_grad = (act_grad * gelu_slope(pre_act)).astype(jnp.bfloat16)
    up_hidden_grad = jnp.einsum(
        "tkg,tkm->kgm", hidden_tiles, pre_grad, preferred_element_type=jnp.float32
    )
    tile_grad = jnp.einsum(
        "tkm,kgm->tkg", pre_grad, up_hidden, preferred_element_type=jnp.float32
    ).astype(jnp.bfloat16)
    portion = lax.all_to_all(tile_grad, "block", split_axis=2, concat_axis=1, tiled=True)
    flattened = portion.reshape(portion.shape[0], block_size * expand)
    tokens_grad = contract_cols(flattened, up_width[0]).astype(jnp.bfloat16)
    up_width_grad = contract_rows(tokens, flattened)[None]
    summed = (
        lax.psum(up_width_grad.astype(jnp.bfloat16), "dp").astype(jnp.float32),
        lax.psum(up_hidden_grad.astype(jnp.bfloat16), "dp").astype(jnp.float32),
        lax.psum(down_hidden_grad.astype(jnp.bfloat16), "dp").astype(jnp.float32),
        lax.psum(down_width_grad.astype(jnp.bfloat16), "dp").astype(jnp.float32),
    )
    results = tuple((member * grad_scale for member in summed))
    return (layer_out, tokens_grad, results[0], results[1], results[2], results[3])


CHUNKS = 4
KEEP = 8
STRIDE = 13


def dot(left, right, left_dim, right_dim):
    return lax.dot_general(
        left,
        right,
        (((left_dim,), (right_dim,)), ((), ())),
        preferred_element_type=jnp.float32,
    )


def fused_kernel(
    n, chunk, scale,
    x_ref, c_ref, uw_ref, uh_ref, dh_ref, dw_ref, swap_ref,
    out_ref, tg_ref, guw_ref, guh_ref, gdh_ref, gdw_ref,
    send_in, recv_in, send_back, recv_back, tiles, rows_back, uw_t, guw_t,
    send_sem, recv_sem,
):
    me = lax.axis_index("block")
    slab = send_in.shape[2] // n
    spread = slab // KEEP
    group_rows = KEEP * slab
    groups = n // KEEP
    part_rows = KEEP * spread

    barrier = pltpu.get_barrier_semaphore()

    def greet(step, carry):
        pl.semaphore_signal(
            barrier,
            inc=1,
            device_id={"block": lax.rem(me + step, n)},
            device_id_type=pl.DeviceIdType.MESH,
        )
        return carry

    lax.fori_loop(1, n, greet, 0)
    uw_t[...] = uw_ref[0].T
    guw_t[...] = jnp.zeros_like(guw_t)
    guh_ref[...] = jnp.zeros_like(guh_ref)
    gdh_ref[...] = jnp.zeros_like(gdh_ref)
    gdw_ref[...] = jnp.zeros_like(gdw_ref)

    def slab_rows(index):
        return pl.ds(pl.multiple_of(index * slab, slab), slab)

    def exchange(stage, j, c, source, target):
        def one(step, carry):
            peer = lax.rem(me + lax.rem(step * STRIDE, n), n)
            pltpu.make_async_remote_copy(
                src_ref=source.at[j, c, slab_rows(peer), :],
                dst_ref=target.at[j, c, slab_rows(me), :],
                send_sem=send_sem.at[stage, j, c],
                recv_sem=recv_sem.at[stage, j, c],
                device_id={"block": peer},
                device_id_type=pl.DeviceIdType.MESH,
            ).start()
            return carry

        lax.fori_loop(1, n, one, 0)
        target[j, c, slab_rows(me), :] = source[j, c, slab_rows(me), :]

    def await_all(ref, j, c, sem):
        part = ref.at[j, c, pl.ds(0, (n - 1) * slab), :]
        pltpu.make_async_copy(part, part, sem).wait()

    def token_rows(c):
        return pl.ds(pl.multiple_of(c * chunk, chunk), chunk)

    def first(c, carry):
        h = dot(uw_t[...], x_ref[token_rows(c), :], 1, 1)
        send_in[0, c] = h.astype(jnp.bfloat16)

        @pl.when(c == 0)
        def _():
            pl.semaphore_wait(barrier, n - 1)

        exchange(0, 0, c, send_in, recv_in)
        df = dot(dw_ref[0], c_ref[token_rows(c), :], 1, 1)
        send_in[1, c] = df.astype(jnp.bfloat16)
        exchange(0, 1, c, send_in, recv_in)
        return carry

    lax.fori_loop(0, CHUNKS, first, 0)

    def hidden(c, carry):
        for j in range(2):
            await_all(recv_in, j, c, recv_sem.at[0, j, c])
            for g in range(groups):
                moved = dot(
                    swap_ref[...], recv_in[j, c, g * group_rows : (g + 1) * group_rows, :], 1, 0
                ).astype(jnp.bfloat16)
                for k in range(KEEP):
                    tiles[j, k, g * part_rows : (g + 1) * part_rows, :] = moved[
                        k * part_rows : (k + 1) * part_rows
                    ]

        def block(k, inner):
            z, de = tiles[0, k], tiles[1, k]
            uh, dh = uh_ref[k], dh_ref[k]
            p = dot(uh, z, 0, 0)
            da = dot(dh, de, 1, 0)
            cdf = 0.5 * (1.0 + lax.erf(p * (1.0 / math.sqrt(2.0))))
            a = (p * cdf).astype(jnp.bfloat16)
            slope = cdf + p * jnp.exp(-0.5 * p * p) * (1.0 / math.sqrt(2.0 * math.pi))
            dp = (da * slope).astype(jnp.bfloat16)
            e = dot(dh, a, 0, 0).astype(jnp.bfloat16)
            dz = dot(uh, dp, 1, 0).astype(jnp.bfloat16)
            gdh_ref[k] += dot(a, de, 1, 1)
            guh_ref[k] += dot(z, dp, 1, 1)
            here = pl.ds(pl.multiple_of(k * part_rows, part_rows), part_rows)
            for g in range(groups):
                rows_back[0, g, here, :] = e[g * part_rows : (g + 1) * part_rows]
                rows_back[1, g, here, :] = dz[g * part_rows : (g + 1) * part_rows]
            return inner

        lax.fori_loop(0, KEEP, block, 0)
        for j in range(2):
            for g in range(groups):
                send_back[j, c, g * group_rows : (g + 1) * group_rows, :] = dot(
                    swap_ref[...], rows_back[j, g], 1, 0
                ).astype(jnp.bfloat16)
            exchange(1, j, c, send_back, recv_back)
        return carry

    lax.fori_loop(0, CHUNKS, hidden, 0)
    guh_ref[...] *= scale
    gdh_ref[...] *= scale

    def last(c, carry):
        here = token_rows(c)
        await_all(recv_back, 0, c, recv_sem.at[1, 0, c])
        f = recv_back[0, c]
        out_ref[here, :] = dot(f, dw_ref[0], 0, 0).astype(jnp.bfloat16)
        gdw_ref[0] += dot(f, c_ref[here, :], 1, 0)
        await_all(recv_back, 1, c, recv_sem.at[1, 1, c])
        dh = recv_back[1, c]
        tg_ref[here, :] = dot(dh, uw_t[...], 0, 0).astype(jnp.bfloat16)
        guw_t[...] += dot(dh, x_ref[here, :], 1, 0)
        return carry

    lax.fori_loop(0, CHUNKS, last, 0)
    gdw_ref[...] *= scale
    guw_ref[0] = guw_t[...].T * scale

    def drain(c, carry):
        for j in range(2):
            await_all(send_in, j, c, send_sem.at[0, j, c])
            await_all(send_back, j, c, send_sem.at[1, j, c])
        return carry

    lax.fori_loop(0, CHUNKS, drain, 0)


def fused(tokens, cotangent, up_width, up_hidden, down_hidden, down_width):
    n = lax.axis_size("block")
    rows, block_size = tokens.shape
    width = up_width.shape[2]
    keep, tile = up_hidden.shape[0], up_hidden.shape[1]
    spread = width // block_size
    chunk = rows // CHUNKS
    group_rows = KEEP * KEEP * spread
    row = jnp.arange(group_rows)
    source = (row // spread % KEEP) * (KEEP * spread) + row // (KEEP * spread) * spread + row % spread
    swap = (source[:, None] == row[None, :]).astype(jnp.bfloat16)
    wide = (2, CHUNKS, width, chunk)
    vmem = pl.BlockSpec(memory_space=pltpu.VMEM)
    shape = jax.ShapeDtypeStruct
    return tuple(
        pl.pallas_call(
            functools.partial(fused_kernel, n, chunk, 1.0 / math.sqrt(rows)),
            out_shape=[
                shape(tokens.shape, jnp.bfloat16),
                shape(tokens.shape, jnp.bfloat16),
                shape(up_width.shape, jnp.float32),
                shape(up_hidden.shape, jnp.float32),
                shape(down_hidden.shape, jnp.float32),
                shape(down_width.shape, jnp.float32),
            ],
            in_specs=[vmem] * 7,
            out_specs=[vmem] * 6,
            scratch_shapes=[
                pltpu.VMEM(wide, jnp.bfloat16),
                pltpu.VMEM(wide, jnp.bfloat16),
                pltpu.VMEM(wide, jnp.bfloat16),
                pltpu.VMEM(wide, jnp.bfloat16),
                pltpu.VMEM((2, keep, tile, chunk), jnp.bfloat16),
                pltpu.VMEM((2, n // KEEP, group_rows, chunk), jnp.bfloat16),
                pltpu.VMEM((width, block_size), jnp.bfloat16),
                pltpu.VMEM((width, block_size), jnp.float32),
                pltpu.SemaphoreType.DMA((2, 2, CHUNKS)),
                pltpu.SemaphoreType.DMA((2, 2, CHUNKS)),
            ],
            compiler_params=pltpu.CompilerParams(
                collective_id=0, has_side_effects=True, vmem_limit_bytes=52 * 1024 * 1024
            ),
        )(tokens, cotangent, up_width, up_hidden, down_hidden, down_width, swap)
    )


def layer(tokens, cotangent, up_width, up_hidden, down_hidden, down_width):
    n = lax.axis_size("block")
    fits = (
        lax.axis_size("dp") == 1
        and n % KEEP == 0
        and math.gcd(STRIDE, n) == 1
        and up_hidden.shape[0] == KEEP
        and tokens.shape[0] % (CHUNKS * 128) == 0
        and tokens.shape[0] <= 1024
    )
    chosen = fused if fits else shards
    return chosen(tokens, cotangent, up_width, up_hidden, down_hidden, down_width)


def solution(mesh):
    in_specs = (
        P("dp", "block"),
        P("dp", "block"),
        P("block", None, None),
        P("block", None, None),
        P("block", None, None),
        P("block", None, None),
    )
    out_specs = (
        P("dp", "block"),
        P("dp", "block"),
        P("block", None, None),
        P("block", None, None),
        P("block", None, None),
        P("block", None, None),
    )
    return jax.shard_map(layer, mesh=mesh, in_specs=in_specs, out_specs=out_specs, check_vma=False)
```

```python
import functools
import math

import jax
import jax.numpy as jnp
from jax import lax
from jax.experimental import pallas as pl
from jax.experimental.pallas import tpu as pltpu
from jax.sharding import PartitionSpec as P


def gelu_exact(value):
    return 0.5 * value * (1.0 + jax.scipy.special.erf(value / math.sqrt(2.0)))


def gelu_slope(value):
    return 0.5 * (1.0 + jax.scipy.special.erf(value / math.sqrt(2.0))) + value * jnp.exp(
        -0.5 * value * value
    ) / math.sqrt(2.0 * math.pi)


def contract_rows(left, right):
    return lax.dot_general(
        left, right, (((0,), (0,)), ((), ())), preferred_element_type=jnp.float32
    )


def contract_cols(left, right):
    return lax.dot_general(
        left, right, (((1,), (1,)), ((), ())), preferred_element_type=jnp.float32
    )


def shards(tokens, cotangent, up_width, up_hidden, down_hidden, down_width):
    row_count = tokens.shape[0]
    block_size = tokens.shape[1]
    expand = up_width.shape[2] // block_size
    grad_scale = 1.0 / math.sqrt(row_count * lax.axis_size("dp"))
    expanded = jnp.dot(tokens, up_width[0], preferred_element_type=jnp.float32).astype(jnp.bfloat16)
    hidden_tiles = lax.all_to_all(
        expanded.reshape(row_count, block_size, expand),
        "block",
        split_axis=1,
        concat_axis=2,
        tiled=True,
    )
    pre_act = jnp.einsum(
        "tkg,kgm->tkm", hidden_tiles, up_hidden, preferred_element_type=jnp.float32
    )
    active = gelu_exact(pre_act).astype(jnp.bfloat16)
    back_rows = jnp.einsum(
        "tkm,kmn->tkn", active, down_hidden, preferred_element_type=jnp.float32
    ).astype(jnp.bfloat16)
    portion = lax.all_to_all(back_rows, "block", split_axis=2, concat_axis=1, tiled=True)
    flattened = portion.reshape(portion.shape[0], block_size * expand)
    gathered_rows = flattened
    layer_out = jnp.dot(flattened, down_width[0], preferred_element_type=jnp.float32).astype(
        jnp.bfloat16
    )
    out_rows_grad = contract_cols(cotangent, down_width[0]).astype(jnp.bfloat16)
    down_width_grad = contract_rows(gathered_rows, cotangent)[None]
    grad_tiles = lax.all_to_all(
        out_rows_grad.reshape(row_count, block_size, expand),
        "block",
        split_axis=1,
        concat_axis=2,
        tiled=True,
    )
    down_hidden_grad = jnp.einsum(
        "tkm,tkn->kmn", active, grad_tiles, preferred_element_type=jnp.float32
    )
    act_grad = jnp.einsum(
        "tkn,kmn->tkm", grad_tiles, down_hidden, preferred_element_type=jnp.float32
    )
    pre_grad = (act_grad * gelu_slope(pre_act)).astype(jnp.bfloat16)
    up_hidden_grad = jnp.einsum(
        "tkg,tkm->kgm", hidden_tiles, pre_grad, preferred_element_type=jnp.float32
    )
    tile_grad = jnp.einsum(
        "tkm,kgm->tkg", pre_grad, up_hidden, preferred_element_type=jnp.float32
    ).astype(jnp.bfloat16)
    portion = lax.all_to_all(tile_grad, "block", split_axis=2, concat_axis=1, tiled=True)
    flattened = portion.reshape(portion.shape[0], block_size * expand)
    tokens_grad = contract_cols(flattened, up_width[0]).astype(jnp.bfloat16)
    up_width_grad = contract_rows(tokens, flattened)[None]
    summed = (
        lax.psum(up_width_grad.astype(jnp.bfloat16), "dp").astype(jnp.float32),
        lax.psum(up_hidden_grad.astype(jnp.bfloat16), "dp").astype(jnp.float32),
        lax.psum(down_hidden_grad.astype(jnp.bfloat16), "dp").astype(jnp.float32),
        lax.psum(down_width_grad.astype(jnp.bfloat16), "dp").astype(jnp.float32),
    )
    results = tuple((member * grad_scale for member in summed))
    return (layer_out, tokens_grad, results[0], results[1], results[2], results[3])


CHUNKS = 4
KEEP = 8
STRIDE = 13


def dot(left, right, left_dim, right_dim):
    return lax.dot_general(
        left,
        right,
        (((left_dim,), (right_dim,)), ((), ())),
        preferred_element_type=jnp.float32,
    )


def fused_kernel(
    n, chunk, scale,
    x_ref, c_ref, uw_ref, uh_ref, dh_ref, dw_ref, swap_ref,
    out_ref, tg_ref, guw_ref, guh_ref, gdh_ref, gdw_ref,
    send_in, recv_in, send_back, recv_back, tiles, rows_back, uw_t, guw_t,
    x_far, c_far, uw_far, dw_far,
    send_sem, recv_sem, row_send, row_recv, weight_send, weight_recv,
):
    me = lax.axis_index("block")
    half = n // 2
    side = me // half
    partner = lax.rem(me + half, n)
    half_rows = send_in.shape[2] // 2
    slab = send_in.shape[2] // n
    spread = slab // KEEP
    group_rows = KEEP * slab
    groups = n // KEEP
    part_rows = KEEP * spread

    barrier = pltpu.get_barrier_semaphore()

    def greet(step, carry):
        pl.semaphore_signal(
            barrier,
            inc=1,
            device_id={"block": lax.rem(me + step, n)},
            device_id_type=pl.DeviceIdType.MESH,
        )
        return carry

    lax.fori_loop(1, n, greet, 0)
    uw_t[...] = uw_ref[0].T
    guw_t[...] = jnp.zeros_like(guw_t)
    guh_ref[...] = jnp.zeros_like(guh_ref)
    gdh_ref[...] = jnp.zeros_like(gdh_ref)
    gdw_ref[...] = jnp.zeros_like(gdw_ref)

    def slab_rows(index):
        return pl.ds(pl.multiple_of(index * slab, slab), slab)

    def token_rows(c):
        return pl.ds(pl.multiple_of(c * chunk, chunk), chunk)

    def half_of(index):
        return pl.ds(pl.multiple_of(index * half_rows, half_rows), half_rows)

    def remote(source, target, sent, received, peer):
        return pltpu.make_async_remote_copy(
            src_ref=source,
            dst_ref=target,
            send_sem=sent,
            recv_sem=received,
            device_id={"block": peer},
            device_id_type=pl.DeviceIdType.MESH,
        )

    def rows_copy(j, c):
        here = token_rows(c)
        source, target = ((x_ref, x_far), (c_ref, c_far))[j]
        return remote(
            source.at[here, :], target.at[here, :], row_send.at[j, c], row_recv.at[j, c], partner
        )

    def weight_copy(j):
        source = (uw_t, dw_ref.at[0])[j].at[half_of(1 - side), :]
        return remote(
            source, (uw_far, dw_far)[j], weight_send.at[j], weight_recv.at[j], partner
        )

    def scatter(j, c, owner, base):
        def one(step, carry):
            place = lax.rem(lax.rem(me, half) + lax.rem(step * STRIDE, half), half)
            remote(
                send_in.at[j, c, pl.ds(pl.multiple_of(base + place * slab, slab), slab), :],
                recv_in.at[j, c, slab_rows(owner), :],
                send_sem.at[0, j, c],
                recv_sem.at[0, j, c],
                side * half + place,
            ).start()
            return carry

        lax.fori_loop(1, half, one, 0)
        mine = pl.ds(pl.multiple_of(base + lax.rem(me, half) * slab, slab), slab)
        recv_in[j, c, slab_rows(owner), :] = send_in[j, c, mine, :]

    def gather(j, c):
        def one(step, carry):
            peer = lax.rem(me + lax.rem(step * STRIDE, n), n)
            remote(
                send_back.at[j, c, slab_rows(peer), :],
                recv_back.at[j, c, slab_rows(me), :],
                send_sem.at[1, j, c],
                recv_sem.at[1, j, c],
                peer,
            ).start()
            return carry

        lax.fori_loop(1, n, one, 0)
        recv_back[j, c, slab_rows(me), :] = send_back[j, c, slab_rows(me), :]

    def await_all(ref, j, c, sem, count):
        part = ref.at[j, c, pl.ds(0, count * slab), :]
        pltpu.make_async_copy(part, part, sem).wait()

    pl.semaphore_wait(barrier, n - 1)
    for j in range(2):
        rows_copy(j, 0).start()
        weight_copy(j).start()

    def first(c):
        @pl.when(c + 1 < CHUNKS)
        def _():
            for j in range(2):
                rows_copy(j, c + 1).start()

        here = token_rows(c)
        near = ((uw_t, x_ref), (dw_ref.at[0], c_ref))
        for j, (weight, rows) in enumerate(near):
            h = dot(weight[half_of(side), :], rows[here, :], 1, 1)
            send_in[j, c, :half_rows, :] = h.astype(jnp.bfloat16)
            scatter(j, c, me, 0)
        far = ((uw_far, x_far), (dw_far, c_far))
        for j, (weight, rows) in enumerate(far):
            rows_copy(j, c).wait_recv()

            @pl.when(c == 0)
            def _():
                weight_copy(j).wait_recv()

            h = dot(weight[...], rows[here, :], 1, 1)
            send_in[j, c, half_rows:, :] = h.astype(jnp.bfloat16)
            scatter(j, c, partner, half_rows)

    def hidden(c):
        for j in range(2):
            await_all(recv_in, j, c, recv_sem.at[0, j, c], n - 2)
            for g in range(groups):
                moved = dot(
                    swap_ref[...], recv_in[j, c, g * group_rows : (g + 1) * group_rows, :], 1, 0
                ).astype(jnp.bfloat16)
                for k in range(KEEP):
                    tiles[j, k, g * part_rows : (g + 1) * part_rows, :] = moved[
                        k * part_rows : (k + 1) * part_rows
                    ]

        def block(k, inner):
            z, de = tiles[0, k], tiles[1, k]
            uh, dh = uh_ref[k], dh_ref[k]
            p = dot(uh, z, 0, 0)
            da = dot(dh, de, 1, 0)
            cdf = 0.5 * (1.0 + lax.erf(p * (1.0 / math.sqrt(2.0))))
            a = (p * cdf).astype(jnp.bfloat16)
            slope = cdf + p * jnp.exp(-0.5 * p * p) * (1.0 / math.sqrt(2.0 * math.pi))
            dp = (da * slope).astype(jnp.bfloat16)
            e = dot(dh, a, 0, 0).astype(jnp.bfloat16)
            dz = dot(uh, dp, 1, 0).astype(jnp.bfloat16)
            gdh_ref[k] += dot(a, de, 1, 1)
            guh_ref[k] += dot(z, dp, 1, 1)
            here = pl.ds(pl.multiple_of(k * part_rows, part_rows), part_rows)
            for g in range(groups):
                rows_back[0, g, here, :] = e[g * part_rows : (g + 1) * part_rows]
                rows_back[1, g, here, :] = dz[g * part_rows : (g + 1) * part_rows]
            return inner

        lax.fori_loop(0, KEEP, block, 0)
        for j in range(2):
            for g in range(groups):
                send_back[j, c, g * group_rows : (g + 1) * group_rows, :] = dot(
                    swap_ref[...], rows_back[j, g], 1, 0
                ).astype(jnp.bfloat16)
            gather(j, c)

    def step(c, carry):
        @pl.when(c < CHUNKS)
        def _():
            first(c)

        @pl.when(c > 0)
        def _():
            hidden(c - 1)

        return carry

    lax.fori_loop(0, CHUNKS + 1, step, 0)
    guh_ref[...] *= scale
    gdh_ref[...] *= scale

    def last(c, carry):
        here = token_rows(c)
        await_all(recv_back, 0, c, recv_sem.at[1, 0, c], n - 1)
        f = recv_back[0, c]
        out_ref[here, :] = dot(f, dw_ref[0], 0, 0).astype(jnp.bfloat16)
        gdw_ref[0] += dot(f, c_ref[here, :], 1, 0)
        await_all(recv_back, 1, c, recv_sem.at[1, 1, c], n - 1)
        dh = recv_back[1, c]
        tg_ref[here, :] = dot(dh, uw_t[...], 0, 0).astype(jnp.bfloat16)
        guw_t[...] += dot(dh, x_ref[here, :], 1, 0)
        return carry

    lax.fori_loop(0, CHUNKS, last, 0)
    gdw_ref[...] *= scale
    guw_ref[0] = guw_t[...].T * scale

    def drain(c, carry):
        for j in range(2):
            await_all(send_in, j, c, send_sem.at[0, j, c], n - 2)
            await_all(send_back, j, c, send_sem.at[1, j, c], n - 1)
            rows_copy(j, c).wait_send()
        return carry

    lax.fori_loop(0, CHUNKS, drain, 0)
    for j in range(2):
        weight_copy(j).wait_send()


def fused(tokens, cotangent, up_width, up_hidden, down_hidden, down_width):
    n = lax.axis_size("block")
    rows, block_size = tokens.shape
    width = up_width.shape[2]
    keep, tile = up_hidden.shape[0], up_hidden.shape[1]
    spread = width // block_size
    chunk = rows // CHUNKS
    group_rows = KEEP * KEEP * spread
    row = jnp.arange(group_rows)
    source = (row // spread % KEEP) * (KEEP * spread) + row // (KEEP * spread) * spread + row % spread
    swap = (source[:, None] == row[None, :]).astype(jnp.bfloat16)
    wide = (2, CHUNKS, width, chunk)
    vmem = pl.BlockSpec(memory_space=pltpu.VMEM)
    shape = jax.ShapeDtypeStruct
    return tuple(
        pl.pallas_call(
            functools.partial(fused_kernel, n, chunk, 1.0 / math.sqrt(rows)),
            out_shape=[
                shape(tokens.shape, jnp.bfloat16),
                shape(tokens.shape, jnp.bfloat16),
                shape(up_width.shape, jnp.float32),
                shape(up_hidden.shape, jnp.float32),
                shape(down_hidden.shape, jnp.float32),
                shape(down_width.shape, jnp.float32),
            ],
            in_specs=[vmem] * 7,
            out_specs=[vmem] * 6,
            scratch_shapes=[
                pltpu.VMEM(wide, jnp.bfloat16),
                pltpu.VMEM(wide, jnp.bfloat16),
                pltpu.VMEM(wide, jnp.bfloat16),
                pltpu.VMEM(wide, jnp.bfloat16),
                pltpu.VMEM((2, keep, tile, chunk), jnp.bfloat16),
                pltpu.VMEM((2, n // KEEP, group_rows, chunk), jnp.bfloat16),
                pltpu.VMEM((width, block_size), jnp.bfloat16),
                pltpu.VMEM((width, block_size), jnp.float32),
                pltpu.VMEM(tokens.shape, jnp.bfloat16),
                pltpu.VMEM(tokens.shape, jnp.bfloat16),
                pltpu.VMEM((width // 2, block_size), jnp.bfloat16),
                pltpu.VMEM((width // 2, block_size), jnp.bfloat16),
                pltpu.SemaphoreType.DMA((2, 2, CHUNKS)),
                pltpu.SemaphoreType.DMA((2, 2, CHUNKS)),
                pltpu.SemaphoreType.DMA((2, CHUNKS)),
                pltpu.SemaphoreType.DMA((2, CHUNKS)),
                pltpu.SemaphoreType.DMA((2,)),
                pltpu.SemaphoreType.DMA((2,)),
            ],
            compiler_params=pltpu.CompilerParams(
                collective_id=0, has_side_effects=True, vmem_limit_bytes=52 * 1024 * 1024
            ),
        )(tokens, cotangent, up_width, up_hidden, down_hidden, down_width, swap)
    )


def layer(tokens, cotangent, up_width, up_hidden, down_hidden, down_width):
    n = lax.axis_size("block")
    fits = (
        lax.axis_size("dp") == 1
        and n % KEEP == 0
        and math.gcd(STRIDE, n) == 1
        and up_hidden.shape[0] == KEEP
        and tokens.shape[0] % (CHUNKS * 128) == 0
        and tokens.shape[0] <= 1024
    )
    chosen = fused if fits else shards
    return chosen(tokens, cotangent, up_width, up_hidden, down_hidden, down_width)


def solution(mesh):
    in_specs = (
        P("dp", "block"),
        P("dp", "block"),
        P("block", None, None),
        P("block", None, None),
        P("block", None, None),
        P("block", None, None),
    )
    out_specs = (
        P("dp", "block"),
        P("dp", "block"),
        P("block", None, None),
        P("block", None, None),
        P("block", None, None),
        P("block", None, None),
    )
    return jax.shard_map(layer, mesh=mesh, in_specs=in_specs, out_specs=out_specs, check_vma=False)
```

```python
import functools
import math

import jax
import jax.numpy as jnp
from jax import lax
from jax.experimental import pallas as pl
from jax.experimental.pallas import tpu as pltpu
from jax.sharding import PartitionSpec as P


def gelu_exact(value):
    return 0.5 * value * (1.0 + jax.scipy.special.erf(value / math.sqrt(2.0)))


def gelu_slope(value):
    return 0.5 * (1.0 + jax.scipy.special.erf(value / math.sqrt(2.0))) + value * jnp.exp(
        -0.5 * value * value
    ) / math.sqrt(2.0 * math.pi)


def contract_rows(left, right):
    return lax.dot_general(
        left, right, (((0,), (0,)), ((), ())), preferred_element_type=jnp.float32
    )


def contract_cols(left, right):
    return lax.dot_general(
        left, right, (((1,), (1,)), ((), ())), preferred_element_type=jnp.float32
    )


def shards(tokens, cotangent, up_width, up_hidden, down_hidden, down_width):
    row_count = tokens.shape[0]
    block_size = tokens.shape[1]
    expand = up_width.shape[2] // block_size
    grad_scale = 1.0 / math.sqrt(row_count * lax.axis_size("dp"))
    expanded = jnp.dot(tokens, up_width[0], preferred_element_type=jnp.float32).astype(jnp.bfloat16)
    hidden_tiles = lax.all_to_all(
        expanded.reshape(row_count, block_size, expand),
        "block",
        split_axis=1,
        concat_axis=2,
        tiled=True,
    )
    pre_act = jnp.einsum(
        "tkg,kgm->tkm", hidden_tiles, up_hidden, preferred_element_type=jnp.float32
    )
    active = gelu_exact(pre_act).astype(jnp.bfloat16)
    back_rows = jnp.einsum(
        "tkm,kmn->tkn", active, down_hidden, preferred_element_type=jnp.float32
    ).astype(jnp.bfloat16)
    portion = lax.all_to_all(back_rows, "block", split_axis=2, concat_axis=1, tiled=True)
    flattened = portion.reshape(portion.shape[0], block_size * expand)
    gathered_rows = flattened
    layer_out = jnp.dot(flattened, down_width[0], preferred_element_type=jnp.float32).astype(
        jnp.bfloat16
    )
    out_rows_grad = contract_cols(cotangent, down_width[0]).astype(jnp.bfloat16)
    down_width_grad = contract_rows(gathered_rows, cotangent)[None]
    grad_tiles = lax.all_to_all(
        out_rows_grad.reshape(row_count, block_size, expand),
        "block",
        split_axis=1,
        concat_axis=2,
        tiled=True,
    )
    down_hidden_grad = jnp.einsum(
        "tkm,tkn->kmn", active, grad_tiles, preferred_element_type=jnp.float32
    )
    act_grad = jnp.einsum(
        "tkn,kmn->tkm", grad_tiles, down_hidden, preferred_element_type=jnp.float32
    )
    pre_grad = (act_grad * gelu_slope(pre_act)).astype(jnp.bfloat16)
    up_hidden_grad = jnp.einsum(
        "tkg,tkm->kgm", hidden_tiles, pre_grad, preferred_element_type=jnp.float32
    )
    tile_grad = jnp.einsum(
        "tkm,kgm->tkg", pre_grad, up_hidden, preferred_element_type=jnp.float32
    ).astype(jnp.bfloat16)
    portion = lax.all_to_all(tile_grad, "block", split_axis=2, concat_axis=1, tiled=True)
    flattened = portion.reshape(portion.shape[0], block_size * expand)
    tokens_grad = contract_cols(flattened, up_width[0]).astype(jnp.bfloat16)
    up_width_grad = contract_rows(tokens, flattened)[None]
    summed = (
        lax.psum(up_width_grad.astype(jnp.bfloat16), "dp").astype(jnp.float32),
        lax.psum(up_hidden_grad.astype(jnp.bfloat16), "dp").astype(jnp.float32),
        lax.psum(down_hidden_grad.astype(jnp.bfloat16), "dp").astype(jnp.float32),
        lax.psum(down_width_grad.astype(jnp.bfloat16), "dp").astype(jnp.float32),
    )
    results = tuple((member * grad_scale for member in summed))
    return (layer_out, tokens_grad, results[0], results[1], results[2], results[3])


CHUNKS = 4
KEEP = 8
STRIDE = 13
AHEAD = 2


def dot(left, right, left_dim, right_dim):
    return lax.dot_general(
        left,
        right,
        (((left_dim,), (right_dim,)), ((), ())),
        preferred_element_type=jnp.float32,
    )


def fused_kernel(
    n, chunk, scale,
    x_ref, c_ref, uw_ref, uh_ref, dh_ref, dw_ref, swap_ref,
    out_ref, tg_ref, guw_ref, guh_ref, gdh_ref, gdw_ref,
    send_in, recv_in, send_back, recv_back, tiles, rows_back, uw_t, guw_t,
    x_far, c_far, uw_far, dw_far,
    send_sem, recv_sem, row_send, row_recv, weight_send, weight_recv,
):
    me = lax.axis_index("block")
    half = n // 2
    side = me // half
    partner = lax.rem(me + half, n)
    half_rows = send_in.shape[2] // 2
    slab = send_in.shape[2] // n
    spread = slab // KEEP
    group_rows = KEEP * slab
    groups = n // KEEP
    part_rows = KEEP * spread

    barrier = pltpu.get_barrier_semaphore()

    def greet(step, carry):
        pl.semaphore_signal(
            barrier,
            inc=1,
            device_id={"block": lax.rem(me + step, n)},
            device_id_type=pl.DeviceIdType.MESH,
        )
        return carry

    lax.fori_loop(1, n, greet, 0)
    uw_t[...] = uw_ref[0].T
    guw_t[...] = jnp.zeros_like(guw_t)
    guh_ref[...] = jnp.zeros_like(guh_ref)
    gdh_ref[...] = jnp.zeros_like(gdh_ref)
    gdw_ref[...] = jnp.zeros_like(gdw_ref)

    def slab_rows(index):
        return pl.ds(pl.multiple_of(index * slab, slab), slab)

    def token_rows(c):
        return pl.ds(pl.multiple_of(c * chunk, chunk), chunk)

    def half_of(index):
        return pl.ds(pl.multiple_of(index * half_rows, half_rows), half_rows)

    def remote(source, target, sent, received, peer):
        return pltpu.make_async_remote_copy(
            src_ref=source,
            dst_ref=target,
            send_sem=sent,
            recv_sem=received,
            device_id={"block": peer},
            device_id_type=pl.DeviceIdType.MESH,
        )

    def rows_copy(j, c):
        here = token_rows(c)
        source, target = ((x_ref, x_far), (c_ref, c_far))[j]
        return remote(
            source.at[here, :], target.at[here, :], row_send.at[j, c], row_recv.at[j, c], partner
        )

    def weight_copy(j):
        source = (uw_t, dw_ref.at[0])[j].at[half_of(1 - side), :]
        return remote(
            source, (uw_far, dw_far)[j], weight_send.at[j], weight_recv.at[j], partner
        )

    def scatter(j, c, owner, base):
        def one(step, carry):
            place = lax.rem(lax.rem(me, half) + lax.rem(step * STRIDE, half), half)
            remote(
                send_in.at[j, c, pl.ds(pl.multiple_of(base + place * slab, slab), slab), :],
                recv_in.at[j, c, slab_rows(owner), :],
                send_sem.at[0, j, c],
                recv_sem.at[0, j, c],
                side * half + place,
            ).start()
            return carry

        lax.fori_loop(1, half, one, 0)
        mine = pl.ds(pl.multiple_of(base + lax.rem(me, half) * slab, slab), slab)
        recv_in[j, c, slab_rows(owner), :] = send_in[j, c, mine, :]

    def gather(j, c):
        def one(step, carry):
            peer = lax.rem(me + lax.rem(step * STRIDE, n), n)
            remote(
                send_back.at[j, c, slab_rows(peer), :],
                recv_back.at[j, c, slab_rows(me), :],
                send_sem.at[1, j, c],
                recv_sem.at[1, j, c],
                peer,
            ).start()
            return carry

        lax.fori_loop(1, n, one, 0)
        recv_back[j, c, slab_rows(me), :] = send_back[j, c, slab_rows(me), :]

    def await_all(ref, j, c, sem, count):
        part = ref.at[j, c, pl.ds(0, count * slab), :]
        pltpu.make_async_copy(part, part, sem).wait()

    pl.semaphore_wait(barrier, n - 1)
    for j in range(2):
        rows_copy(j, 0).start()
        weight_copy(j).start()
    for ahead in range(1, AHEAD):
        for j in range(2):
            rows_copy(j, ahead).start()

    def first(c):
        @pl.when(c + AHEAD < CHUNKS)
        def _():
            for j in range(2):
                rows_copy(j, c + AHEAD).start()

        here = token_rows(c)
        near = ((uw_t, x_ref), (dw_ref.at[0], c_ref))
        for j, (weight, rows) in enumerate(near):
            h = dot(weight[half_of(side), :], rows[here, :], 1, 1)
            send_in[j, c, :half_rows, :] = h.astype(jnp.bfloat16)
            scatter(j, c, me, 0)
        far = ((uw_far, x_far), (dw_far, c_far))
        for j, (weight, rows) in enumerate(far):
            rows_copy(j, c).wait_recv()

            @pl.when(c == 0)
            def _():
                weight_copy(j).wait_recv()

            h = dot(weight[...], rows[here, :], 1, 1)
            send_in[j, c, half_rows:, :] = h.astype(jnp.bfloat16)
            scatter(j, c, partner, half_rows)

    def hidden(c):
        for j in range(2):
            await_all(recv_in, j, c, recv_sem.at[0, j, c], n - 2)
            for g in range(groups):
                moved = dot(
                    swap_ref[...], recv_in[j, c, g * group_rows : (g + 1) * group_rows, :], 1, 0
                ).astype(jnp.bfloat16)
                for k in range(KEEP):
                    tiles[j, k, g * part_rows : (g + 1) * part_rows, :] = moved[
                        k * part_rows : (k + 1) * part_rows
                    ]

        def block(k, inner):
            z, de = tiles[0, k], tiles[1, k]
            uh, dh = uh_ref[k], dh_ref[k]
            p = dot(uh, z, 0, 0)
            da = dot(dh, de, 1, 0)
            cdf = 0.5 * (1.0 + lax.erf(p * (1.0 / math.sqrt(2.0))))
            a = (p * cdf).astype(jnp.bfloat16)
            slope = cdf + p * jnp.exp(-0.5 * p * p) * (1.0 / math.sqrt(2.0 * math.pi))
            dp = (da * slope).astype(jnp.bfloat16)
            e = dot(dh, a, 0, 0).astype(jnp.bfloat16)
            dz = dot(uh, dp, 1, 0).astype(jnp.bfloat16)
            gdh_ref[k] += dot(a, de, 1, 1)
            guh_ref[k] += dot(z, dp, 1, 1)
            here = pl.ds(pl.multiple_of(k * part_rows, part_rows), part_rows)
            for g in range(groups):
                rows_back[0, g, here, :] = e[g * part_rows : (g + 1) * part_rows]
                rows_back[1, g, here, :] = dz[g * part_rows : (g + 1) * part_rows]
            return inner

        lax.fori_loop(0, KEEP, block, 0)
        for j in range(2):
            for g in range(groups):
                send_back[j, c, g * group_rows : (g + 1) * group_rows, :] = dot(
                    swap_ref[...], rows_back[j, g], 1, 0
                ).astype(jnp.bfloat16)
            gather(j, c)

    def step(c, carry):
        @pl.when(c < CHUNKS)
        def _():
            first(c)

        @pl.when(c > 0)
        def _():
            hidden(c - 1)

        return carry

    lax.fori_loop(0, CHUNKS + 1, step, 0)
    guh_ref[...] *= scale
    gdh_ref[...] *= scale

    def last(c, carry):
        here = token_rows(c)
        await_all(recv_back, 0, c, recv_sem.at[1, 0, c], n - 1)
        f = recv_back[0, c]
        out_ref[here, :] = dot(f, dw_ref[0], 0, 0).astype(jnp.bfloat16)
        gdw_ref[0] += dot(f, c_ref[here, :], 1, 0)
        await_all(recv_back, 1, c, recv_sem.at[1, 1, c], n - 1)
        dh = recv_back[1, c]
        tg_ref[here, :] = dot(dh, uw_t[...], 0, 0).astype(jnp.bfloat16)
        guw_t[...] += dot(dh, x_ref[here, :], 1, 0)
        return carry

    lax.fori_loop(0, CHUNKS, last, 0)
    gdw_ref[...] *= scale
    guw_ref[0] = guw_t[...].T * scale

    def drain(c, carry):
        for j in range(2):
            await_all(send_in, j, c, send_sem.at[0, j, c], n - 2)
            await_all(send_back, j, c, send_sem.at[1, j, c], n - 1)
            rows_copy(j, c).wait_send()
        return carry

    lax.fori_loop(0, CHUNKS, drain, 0)
    for j in range(2):
        weight_copy(j).wait_send()


def fused(tokens, cotangent, up_width, up_hidden, down_hidden, down_width):
    n = lax.axis_size("block")
    rows, block_size = tokens.shape
    width = up_width.shape[2]
    keep, tile = up_hidden.shape[0], up_hidden.shape[1]
    spread = width // block_size
    chunk = rows // CHUNKS
    group_rows = KEEP * KEEP * spread
    row = jnp.arange(group_rows)
    source = (row // spread % KEEP) * (KEEP * spread) + row // (KEEP * spread) * spread + row % spread
    swap = (source[:, None] == row[None, :]).astype(jnp.bfloat16)
    wide = (2, CHUNKS, width, chunk)
    vmem = pl.BlockSpec(memory_space=pltpu.VMEM)
    shape = jax.ShapeDtypeStruct
    return tuple(
        pl.pallas_call(
            functools.partial(fused_kernel, n, chunk, 1.0 / math.sqrt(rows)),
            out_shape=[
                shape(tokens.shape, jnp.bfloat16),
                shape(tokens.shape, jnp.bfloat16),
                shape(up_width.shape, jnp.float32),
                shape(up_hidden.shape, jnp.float32),
                shape(down_hidden.shape, jnp.float32),
                shape(down_width.shape, jnp.float32),
            ],
            in_specs=[vmem] * 7,
            out_specs=[vmem] * 6,
            scratch_shapes=[
                pltpu.VMEM(wide, jnp.bfloat16),
                pltpu.VMEM(wide, jnp.bfloat16),
                pltpu.VMEM(wide, jnp.bfloat16),
                pltpu.VMEM(wide, jnp.bfloat16),
                pltpu.VMEM((2, keep, tile, chunk), jnp.bfloat16),
                pltpu.VMEM((2, n // KEEP, group_rows, chunk), jnp.bfloat16),
                pltpu.VMEM((width, block_size), jnp.bfloat16),
                pltpu.VMEM((width, block_size), jnp.float32),
                pltpu.VMEM(tokens.shape, jnp.bfloat16),
                pltpu.VMEM(tokens.shape, jnp.bfloat16),
                pltpu.VMEM((width // 2, block_size), jnp.bfloat16),
                pltpu.VMEM((width // 2, block_size), jnp.bfloat16),
                pltpu.SemaphoreType.DMA((2, 2, CHUNKS)),
                pltpu.SemaphoreType.DMA((2, 2, CHUNKS)),
                pltpu.SemaphoreType.DMA((2, CHUNKS)),
                pltpu.SemaphoreType.DMA((2, CHUNKS)),
                pltpu.SemaphoreType.DMA((2,)),
                pltpu.SemaphoreType.DMA((2,)),
            ],
            compiler_params=pltpu.CompilerParams(
                collective_id=0, has_side_effects=True, vmem_limit_bytes=52 * 1024 * 1024
            ),
        )(tokens, cotangent, up_width, up_hidden, down_hidden, down_width, swap)
    )


def layer(tokens, cotangent, up_width, up_hidden, down_hidden, down_width):
    n = lax.axis_size("block")
    fits = (
        lax.axis_size("dp") == 1
        and n % KEEP == 0
        and math.gcd(STRIDE, n) == 1
        and up_hidden.shape[0] == KEEP
        and tokens.shape[0] % (CHUNKS * 128) == 0
        and tokens.shape[0] <= 1024
    )
    chosen = fused if fits else shards
    return chosen(tokens, cotangent, up_width, up_hidden, down_hidden, down_width)


def solution(mesh):
    in_specs = (
        P("dp", "block"),
        P("dp", "block"),
        P("block", None, None),
        P("block", None, None),
        P("block", None, None),
        P("block", None, None),
    )
    out_specs = (
        P("dp", "block"),
        P("dp", "block"),
        P("block", None, None),
        P("block", None, None),
        P("block", None, None),
        P("block", None, None),
    )
    return jax.shard_map(layer, mesh=mesh, in_specs=in_specs, out_specs=out_specs, check_vma=False)
```

```python
import functools
import math

import jax
import jax.numpy as jnp
from jax import lax
from jax.experimental import pallas as pl
from jax.experimental.pallas import tpu as pltpu
from jax.sharding import PartitionSpec as P


def gelu_exact(value):
    return 0.5 * value * (1.0 + jax.scipy.special.erf(value / math.sqrt(2.0)))


def gelu_slope(value):
    return 0.5 * (1.0 + jax.scipy.special.erf(value / math.sqrt(2.0))) + value * jnp.exp(
        -0.5 * value * value
    ) / math.sqrt(2.0 * math.pi)


def contract_rows(left, right):
    return lax.dot_general(
        left, right, (((0,), (0,)), ((), ())), preferred_element_type=jnp.float32
    )


def contract_cols(left, right):
    return lax.dot_general(
        left, right, (((1,), (1,)), ((), ())), preferred_element_type=jnp.float32
    )


def shards(tokens, cotangent, up_width, up_hidden, down_hidden, down_width):
    row_count = tokens.shape[0]
    block_size = tokens.shape[1]
    expand = up_width.shape[2] // block_size
    grad_scale = 1.0 / math.sqrt(row_count * lax.axis_size("dp"))
    expanded = jnp.dot(tokens, up_width[0], preferred_element_type=jnp.float32).astype(jnp.bfloat16)
    hidden_tiles = lax.all_to_all(
        expanded.reshape(row_count, block_size, expand),
        "block",
        split_axis=1,
        concat_axis=2,
        tiled=True,
    )
    pre_act = jnp.einsum(
        "tkg,kgm->tkm", hidden_tiles, up_hidden, preferred_element_type=jnp.float32
    )
    active = gelu_exact(pre_act).astype(jnp.bfloat16)
    back_rows = jnp.einsum(
        "tkm,kmn->tkn", active, down_hidden, preferred_element_type=jnp.float32
    ).astype(jnp.bfloat16)
    portion = lax.all_to_all(back_rows, "block", split_axis=2, concat_axis=1, tiled=True)
    flattened = portion.reshape(portion.shape[0], block_size * expand)
    gathered_rows = flattened
    layer_out = jnp.dot(flattened, down_width[0], preferred_element_type=jnp.float32).astype(
        jnp.bfloat16
    )
    out_rows_grad = contract_cols(cotangent, down_width[0]).astype(jnp.bfloat16)
    down_width_grad = contract_rows(gathered_rows, cotangent)[None]
    grad_tiles = lax.all_to_all(
        out_rows_grad.reshape(row_count, block_size, expand),
        "block",
        split_axis=1,
        concat_axis=2,
        tiled=True,
    )
    down_hidden_grad = jnp.einsum(
        "tkm,tkn->kmn", active, grad_tiles, preferred_element_type=jnp.float32
    )
    act_grad = jnp.einsum(
        "tkn,kmn->tkm", grad_tiles, down_hidden, preferred_element_type=jnp.float32
    )
    pre_grad = (act_grad * gelu_slope(pre_act)).astype(jnp.bfloat16)
    up_hidden_grad = jnp.einsum(
        "tkg,tkm->kgm", hidden_tiles, pre_grad, preferred_element_type=jnp.float32
    )
    tile_grad = jnp.einsum(
        "tkm,kgm->tkg", pre_grad, up_hidden, preferred_element_type=jnp.float32
    ).astype(jnp.bfloat16)
    portion = lax.all_to_all(tile_grad, "block", split_axis=2, concat_axis=1, tiled=True)
    flattened = portion.reshape(portion.shape[0], block_size * expand)
    tokens_grad = contract_cols(flattened, up_width[0]).astype(jnp.bfloat16)
    up_width_grad = contract_rows(tokens, flattened)[None]
    summed = (
        lax.psum(up_width_grad.astype(jnp.bfloat16), "dp").astype(jnp.float32),
        lax.psum(up_hidden_grad.astype(jnp.bfloat16), "dp").astype(jnp.float32),
        lax.psum(down_hidden_grad.astype(jnp.bfloat16), "dp").astype(jnp.float32),
        lax.psum(down_width_grad.astype(jnp.bfloat16), "dp").astype(jnp.float32),
    )
    results = tuple((member * grad_scale for member in summed))
    return (layer_out, tokens_grad, results[0], results[1], results[2], results[3])


CHUNKS = 4
KEEP = 8
STRIDE = 13


def dot(left, right, left_dim, right_dim):
    return lax.dot_general(
        left,
        right,
        (((left_dim,), (right_dim,)), ((), ())),
        preferred_element_type=jnp.float32,
    )


def fused_kernel(
    n, chunk, scale,
    x_ref, c_ref, uw_ref, uh_ref, dh_ref, dw_ref, swap_ref,
    out_ref, tg_ref, guw_ref, guh_ref, gdh_ref, gdw_ref,
    send_in, recv_in, send_back, recv_back, tiles, acts, slopes, rows_back, uw_t, guw_t,
    x_far, c_far, uw_far, dw_far,
    send_sem, recv_sem, row_send, row_recv, weight_send, weight_recv,
):
    me = lax.axis_index("block")
    half = n // 2
    side = me // half
    partner = lax.rem(me + half, n)
    half_rows = send_in.shape[2] // 2
    slab = send_in.shape[2] // n
    spread = slab // KEEP
    group_rows = KEEP * slab
    groups = n // KEEP
    part_rows = KEEP * spread

    barrier = pltpu.get_barrier_semaphore()

    def greet(step, carry):
        pl.semaphore_signal(
            barrier,
            inc=1,
            device_id={"block": lax.rem(me + step, n)},
            device_id_type=pl.DeviceIdType.MESH,
        )
        return carry

    lax.fori_loop(1, n, greet, 0)
    uw_t[...] = uw_ref[0].T
    guw_t[...] = jnp.zeros_like(guw_t)
    guh_ref[...] = jnp.zeros_like(guh_ref)
    gdh_ref[...] = jnp.zeros_like(gdh_ref)
    gdw_ref[...] = jnp.zeros_like(gdw_ref)

    def slab_rows(index):
        return pl.ds(pl.multiple_of(index * slab, slab), slab)

    def token_rows(c):
        return pl.ds(pl.multiple_of(c * chunk, chunk), chunk)

    def half_of(index):
        return pl.ds(pl.multiple_of(index * half_rows, half_rows), half_rows)

    def remote(source, target, sent, received, peer):
        return pltpu.make_async_remote_copy(
            src_ref=source,
            dst_ref=target,
            send_sem=sent,
            recv_sem=received,
            device_id={"block": peer},
            device_id_type=pl.DeviceIdType.MESH,
        )

    def rows_copy(j, c):
        here = token_rows(c)
        source, target = ((x_ref, x_far), (c_ref, c_far))[j]
        return remote(
            source.at[here, :], target.at[here, :], row_send.at[j, c], row_recv.at[j, c], partner
        )

    def weight_copy(j):
        source = (uw_t, dw_ref.at[0])[j].at[half_of(1 - side), :]
        return remote(
            source, (uw_far, dw_far)[j], weight_send.at[j], weight_recv.at[j], partner
        )

    def scatter(j, c, owner, base):
        def one(step, carry):
            place = lax.rem(lax.rem(me, half) + lax.rem(step * STRIDE, half), half)
            remote(
                send_in.at[j, c, pl.ds(pl.multiple_of(base + place * slab, slab), slab), :],
                recv_in.at[j, c, slab_rows(owner), :],
                send_sem.at[0, j, c],
                recv_sem.at[0, j, c],
                side * half + place,
            ).start()
            return carry

        lax.fori_loop(1, half, one, 0)
        mine = pl.ds(pl.multiple_of(base + lax.rem(me, half) * slab, slab), slab)
        recv_in[j, c, slab_rows(owner), :] = send_in[j, c, mine, :]

    def gather(j, c):
        def one(step, carry):
            peer = lax.rem(me + lax.rem(step * STRIDE, n), n)
            remote(
                send_back.at[j, c, slab_rows(peer), :],
                recv_back.at[j, c, slab_rows(me), :],
                send_sem.at[1, j, c],
                recv_sem.at[1, j, c],
                peer,
            ).start()
            return carry

        lax.fori_loop(1, n, one, 0)
        recv_back[j, c, slab_rows(me), :] = send_back[j, c, slab_rows(me), :]

    def await_all(ref, j, c, sem, count):
        part = ref.at[j, c, pl.ds(0, count * slab), :]
        pltpu.make_async_copy(part, part, sem).wait()

    pl.semaphore_wait(barrier, n - 1)
    for j in range(2):
        rows_copy(j, 0).start()
        weight_copy(j).start()

    def first(c):
        @pl.when(c + 1 < CHUNKS)
        def _():
            for j in range(2):
                rows_copy(j, c + 1).start()

        here = token_rows(c)
        near = ((uw_t, x_ref), (dw_ref.at[0], c_ref))
        for j, (weight, rows) in enumerate(near):
            h = dot(weight[half_of(side), :], rows[here, :], 1, 1)
            send_in[j, c, :half_rows, :] = h.astype(jnp.bfloat16)
            scatter(j, c, me, 0)
        far = ((uw_far, x_far), (dw_far, c_far))
        for j, (weight, rows) in enumerate(far):
            rows_copy(j, c).wait_recv()

            @pl.when(c == 0)
            def _():
                weight_copy(j).wait_recv()

            h = dot(weight[...], rows[here, :], 1, 1)
            send_in[j, c, half_rows:, :] = h.astype(jnp.bfloat16)
            scatter(j, c, partner, half_rows)

    def hidden(c):
        def arrive(j):
            await_all(recv_in, j, c, recv_sem.at[0, j, c], n - 2)
            for g in range(groups):
                moved = dot(
                    swap_ref[...], recv_in[j, c, g * group_rows : (g + 1) * group_rows, :], 1, 0
                ).astype(jnp.bfloat16)
                for k in range(KEEP):
                    tiles[j, k, g * part_rows : (g + 1) * part_rows, :] = moved[
                        k * part_rows : (k + 1) * part_rows
                    ]

        def put(j, k, value):
            here = pl.ds(pl.multiple_of(k * part_rows, part_rows), part_rows)
            for g in range(groups):
                rows_back[j, g, here, :] = value[g * part_rows : (g + 1) * part_rows]

        def leave(j):
            for g in range(groups):
                send_back[j, c, g * group_rows : (g + 1) * group_rows, :] = dot(
                    swap_ref[...], rows_back[j, g], 1, 0
                ).astype(jnp.bfloat16)
            gather(j, c)

        def forward(k, inner):
            p = dot(uh_ref[k], tiles[0, k], 0, 0)
            cdf = 0.5 * (1.0 + lax.erf(p * (1.0 / math.sqrt(2.0))))
            a = (p * cdf).astype(jnp.bfloat16)
            slopes[k] = cdf + p * jnp.exp(-0.5 * p * p) * (1.0 / math.sqrt(2.0 * math.pi))
            acts[0, k] = a
            put(0, k, dot(dh_ref[k], a, 0, 0).astype(jnp.bfloat16))
            return inner

        def backward(k, inner):
            dp = (dot(dh_ref[k], tiles[1, k], 1, 0) * slopes[k]).astype(jnp.bfloat16)
            acts[1, k] = dp
            put(1, k, dot(uh_ref[k], dp, 1, 0).astype(jnp.bfloat16))
            return inner

        def gradients(k, inner):
            gdh_ref[k] += dot(acts[0, k], tiles[1, k], 1, 1)
            guh_ref[k] += dot(tiles[0, k], acts[1, k], 1, 1)
            return inner

        arrive(0)
        lax.fori_loop(0, KEEP, forward, 0)
        leave(0)
        arrive(1)
        lax.fori_loop(0, KEEP, backward, 0)
        leave(1)
        lax.fori_loop(0, KEEP, gradients, 0)

    def step(c, carry):
        @pl.when(c < CHUNKS)
        def _():
            first(c)

        @pl.when(c > 0)
        def _():
            hidden(c - 1)

        return carry

    lax.fori_loop(0, CHUNKS + 1, step, 0)
    guh_ref[...] *= scale
    gdh_ref[...] *= scale

    def last(c, carry):
        here = token_rows(c)
        await_all(recv_back, 0, c, recv_sem.at[1, 0, c], n - 1)
        f = recv_back[0, c]
        out_ref[here, :] = dot(f, dw_ref[0], 0, 0).astype(jnp.bfloat16)
        gdw_ref[0] += dot(f, c_ref[here, :], 1, 0)
        await_all(recv_back, 1, c, recv_sem.at[1, 1, c], n - 1)
        dh = recv_back[1, c]
        tg_ref[here, :] = dot(dh, uw_t[...], 0, 0).astype(jnp.bfloat16)
        guw_t[...] += dot(dh, x_ref[here, :], 1, 0)
        return carry

    lax.fori_loop(0, CHUNKS, last, 0)
    gdw_ref[...] *= scale
    guw_ref[0] = guw_t[...].T * scale

    def drain(c, carry):
        for j in range(2):
            await_all(send_in, j, c, send_sem.at[0, j, c], n - 2)
            await_all(send_back, j, c, send_sem.at[1, j, c], n - 1)
            rows_copy(j, c).wait_send()
        return carry

    lax.fori_loop(0, CHUNKS, drain, 0)
    for j in range(2):
        weight_copy(j).wait_send()


def place_kernel(*refs):
    count = (len(refs) - 1) // 2
    sems = refs[-1]
    copies = [
        pltpu.make_async_copy(refs[item], refs[count + item], sems.at[item])
        for item in range(count)
    ]
    for copy in copies:
        copy.start()
    for copy in copies:
        copy.wait()


def place(arrays):
    anywhere = pl.BlockSpec(memory_space=pl.ANY)
    return tuple(
        pl.pallas_call(
            place_kernel,
            out_shape=[jax.ShapeDtypeStruct(item.shape, item.dtype) for item in arrays],
            in_specs=[anywhere] * len(arrays),
            out_specs=[anywhere] * len(arrays),
            scratch_shapes=[pltpu.SemaphoreType.DMA((len(arrays),))],
        )(*arrays)
    )


def fused(tokens, cotangent, up_width, up_hidden, down_hidden, down_width):
    n = lax.axis_size("block")
    rows, block_size = tokens.shape
    width = up_width.shape[2]
    keep, tile = up_hidden.shape[0], up_hidden.shape[1]
    spread = width // block_size
    chunk = rows // CHUNKS
    group_rows = KEEP * KEEP * spread
    row = jnp.arange(group_rows)
    source = (row // spread % KEEP) * (KEEP * spread) + row // (KEEP * spread) * spread + row % spread
    swap = (source[:, None] == row[None, :]).astype(jnp.bfloat16)
    wide = (2, CHUNKS, width, chunk)
    vmem = pl.BlockSpec(memory_space=pltpu.VMEM)
    shape = jax.ShapeDtypeStruct
    return place(
        pl.pallas_call(
            functools.partial(fused_kernel, n, chunk, 1.0 / math.sqrt(rows)),
            out_shape=[
                shape(tokens.shape, jnp.bfloat16),
                shape(tokens.shape, jnp.bfloat16),
                shape(up_width.shape, jnp.float32),
                shape(up_hidden.shape, jnp.float32),
                shape(down_hidden.shape, jnp.float32),
                shape(down_width.shape, jnp.float32),
            ],
            in_specs=[vmem] * 7,
            out_specs=[vmem] * 6,
            scratch_shapes=[
                pltpu.VMEM(wide, jnp.bfloat16),
                pltpu.VMEM(wide, jnp.bfloat16),
                pltpu.VMEM(wide, jnp.bfloat16),
                pltpu.VMEM(wide, jnp.bfloat16),
                pltpu.VMEM((2, keep, tile, chunk), jnp.bfloat16),
                pltpu.VMEM((2, keep, tile, chunk), jnp.bfloat16),
                pltpu.VMEM((keep, tile, chunk), jnp.float32),
                pltpu.VMEM((2, n // KEEP, group_rows, chunk), jnp.bfloat16),
                pltpu.VMEM((width, block_size), jnp.bfloat16),
                pltpu.VMEM((width, block_size), jnp.float32),
                pltpu.VMEM(tokens.shape, jnp.bfloat16),
                pltpu.VMEM(tokens.shape, jnp.bfloat16),
                pltpu.VMEM((width // 2, block_size), jnp.bfloat16),
                pltpu.VMEM((width // 2, block_size), jnp.bfloat16),
                pltpu.SemaphoreType.DMA((2, 2, CHUNKS)),
                pltpu.SemaphoreType.DMA((2, 2, CHUNKS)),
                pltpu.SemaphoreType.DMA((2, CHUNKS)),
                pltpu.SemaphoreType.DMA((2, CHUNKS)),
                pltpu.SemaphoreType.DMA((2,)),
                pltpu.SemaphoreType.DMA((2,)),
            ],
            compiler_params=pltpu.CompilerParams(
                collective_id=0, has_side_effects=True, vmem_limit_bytes=52 * 1024 * 1024
            ),
        )(tokens, cotangent, up_width, up_hidden, down_hidden, down_width, swap)
    )


def layer(tokens, cotangent, up_width, up_hidden, down_hidden, down_width):
    n = lax.axis_size("block")
    fits = (
        lax.axis_size("dp") == 1
        and n % KEEP == 0
        and math.gcd(STRIDE, n) == 1
        and up_hidden.shape[0] == KEEP
        and tokens.shape[0] % (CHUNKS * 128) == 0
        and tokens.shape[0] <= 1024
    )
    chosen = fused if fits else shards
    return chosen(tokens, cotangent, up_width, up_hidden, down_hidden, down_width)


def solution(mesh):
    in_specs = (
        P("dp", "block"),
        P("dp", "block"),
        P("block", None, None),
        P("block", None, None),
        P("block", None, None),
        P("block", None, None),
    )
    out_specs = (
        P("dp", "block"),
        P("dp", "block"),
        P("block", None, None),
        P("block", None, None),
        P("block", None, None),
        P("block", None, None),
    )
    return jax.shard_map(layer, mesh=mesh, in_specs=in_specs, out_specs=out_specs, check_vma=False)
```
